32 devices in a mesh: groups: 2 (over y), seq: 4 (over z), tensor: 2 (over x), dp: 2 (over core).
Axes of the slice: x: 2, y: 2, z: 4, core: 2. Of those that a mesh axis runs over, the one named last changes fastest.
Arguments:
- inputs: bfloat16 [4, 2048, 2048], P(('groups', 'dp'), 'seq', 'tensor'), parts along dimension 0, may hold values from -6 to 6
- targets: bfloat16 [4, 2048, 2048], P(('groups', 'dp'), 'seq', 'tensor'), parts along dimension 0, may hold values from -6 to 6
- active: int32 [4, 2048], P(('groups', 'dp'), 'seq'), parts along dimension 0, may hold values 0 or 1
- lengths: int32 [4], P(('groups', 'dp')), parts along dimension 0, may hold values from 512 to 2048, as said below
- b_values: bfloat16 [4, 2048, 1024], P(('groups', 'dp'), 'seq', 'tensor'), parts along dimension 0, may hold values from -0.359375 to 0.359375
- c_values: bfloat16 [4, 2048, 1024], P(('groups', 'dp'), 'seq', 'tensor'), parts along dimension 0, may hold values from -0.359375 to 0.359375
- step_sizes: float32 [4, 64, 2048], P(('groups', 'dp'), 'tensor', 'seq'), parts along dimension 0, may hold values from 0.1 to 2
- decay_rates: float32 [64], P('tensor'), may hold values from 4.8828126e-05 to 0.03
- in_weight: bfloat16 [2048, 4096], P(None, 'tensor'), may hold values from -0.125 to 0.125
- out_weight: bfloat16 [4096, 2048], P('tensor'), may hold values from -0.09375 to 0.09375
Outputs:
- grad_inputs: bfloat16 [4, 2048, 2048], P(('groups', 'dp'), 'seq', 'tensor'), parts along dimension 0
- grad_b: float32 [4, 2048, 1024], P(('groups', 'dp'), 'seq', 'tensor'), parts along dimension 0
- grad_c: float32 [4, 2048, 1024], P(('groups', 'dp'), 'seq', 'tensor'), parts along dimension 0
- grad_steps: float32 [4, 64, 2048], P(('groups', 'dp'), 'tensor', 'seq'), parts along dimension 0
- grad_rates: float32 [128], P(('groups', 'tensor')), parts along dimension 0
The draws below stay inside these ranges and needn't reach their ends.
There are 2 independent parts, one for each index of `groups`. The reference program is written for one: setup_inputs(seed, part) draws one part's arguments, and reference() takes and returns one part's arrays. A program takes and returns all parts, laid end to end along the dimension named above; an argument that names none is the same for every part. Nothing has to cross between parts.
Inputs may be any that keep to these rules, and one draw needn't show every extreme that they name: `lengths`: at least one transcript has all 2048 positions valid.
All inputs are finite; a program needn't handle non-finite values. No bound on the sum of `active` on one device may be relied on, other than what follows from the above.
Results may differ from the reference program's by a relative error of at most 0.0065.
Values may be sent and summed in bfloat16 or wider, within the bound.
A program may use at most 256 MiB of HBM per device.

```python
import math
import jax
import jax.numpy as jnp
from jax import lax

D = 2048
HEADS = 64
HEAD_SIZE = 64
STATE = 128
HEAD_GROUPS = 8
TOK_DEV = 512
TRANSCRIPTS = 2
LENGTH = 2048


def draw_lengths(key, part):
    first, second = jax.random.split(jax.random.fold_in(key, 7))
    drawn = jax.random.randint(first, (TRANSCRIPTS,), TOK_DEV, LENGTH + 1)
    chosen = jax.random.randint(second, (), 0, TRANSCRIPTS)
    return jnp.where(jnp.arange(TRANSCRIPTS) == chosen, LENGTH, drawn).astype(jnp.int32)


def plant(entries, stream_key, least, top_value):
    index_at = [jax.random.randint(jax.random.fold_in(stream_key, axis), (), 0, length) for axis, length in enumerate(entries.shape)]
    longest = entries.shape.index(max(entries.shape))
    neighbour = index_at[:longest] + [(index_at[longest] + 1) % entries.shape[longest]] + index_at[longest + 1:]
    return entries.at[tuple(index_at)].set(least).at[tuple(neighbour)].set(top_value)


def block_levels(own_key, extent, pieces, low, largest):
    def one(dim, blocks):
        draws = jax.random.uniform(jax.random.fold_in(jax.random.fold_in(own_key, 6), dim), (blocks,), jnp.float32, low / len(pieces), largest / len(pieces))
        return jnp.repeat(jnp.exp(draws), extent[dim] // blocks).reshape((-1,) + (1,) * (len(extent) - dim - 1))

    gain = one(*pieces[0])
    for cut in pieces[1:]:
        gain = gain * one(*cut)
    return gain


def centred(own_key, dims, deviation, bound, shards=(), held_as=jnp.bfloat16):
    loudness = block_levels(own_key, dims, shards, -0.22, 0.18) if shards else 1.0
    entries = jax.random.normal(own_key, dims, jnp.float32) * deviation * loudness
    return jnp.minimum(jnp.maximum(entries, -bound), bound).astype(held_as)


def setup_inputs(seed: int = 0, part: int = 0) -> dict:
    streams_of = jax.random.split(jax.random.key(seed), 11)
    part_keys = jax.random.split(jax.random.fold_in(streams_of[10], part), 11)
    inputs = centred(part_keys[0], (TRANSCRIPTS, LENGTH, D), 1.0, 6.0, ((0, 2), (1, 4), (2, 2)))
    targets = centred(part_keys[1], (TRANSCRIPTS, LENGTH, D), 1.0, 6.0, ((0, 2), (1, 4), (2, 2)))
    active = plant((jax.random.randint(part_keys[2], (TRANSCRIPTS, LENGTH), 0, 2) < 1).astype(jnp.int32), jax.random.fold_in(part_keys[2], 1), 0, 1)
    lengths = draw_lengths(jax.random.fold_in(jax.random.fold_in(streams_of[10], part), 71), part)
    b_values = centred(part_keys[4], (TRANSCRIPTS, LENGTH, HEAD_GROUPS * STATE), 0.06, 0.359375, ((0, 2), (1, 4), (2, 2)))
    c_values = centred(part_keys[5], (TRANSCRIPTS, LENGTH, HEAD_GROUPS * STATE), 0.06, 0.359375, ((0, 2), (1, 4), (2, 2)))
    step_sizes = jnp.clip(jnp.exp(math.log(2.0) - 2.9957323 * jax.random.uniform(part_keys[6], (TRANSCRIPTS, HEADS, LENGTH), jnp.float32) ** block_levels(part_keys[6], (TRANSCRIPTS, HEADS, LENGTH), ((0, 2), (1, 2), (2, 4)), -0.2, 0.2)), 0.1, 2.0)
    decay_rates = jnp.clip(jnp.exp(math.log(0.03) - 6.420646 * jax.random.uniform(streams_of[7], (HEADS,), jnp.float32) ** block_levels(streams_of[7], (HEADS,), ((0, 2),), -0.2, 0.2)), 4.882812572759576e-05, 0.03)
    in_weight = centred(streams_of[8], (D, HEADS * HEAD_SIZE), D ** -0.5, 0.125, ((1, 2),))
    out_weight = centred(streams_of[9], (HEADS * HEAD_SIZE, D), (HEADS * HEAD_SIZE) ** -0.5, 0.09375, ((0, 2),))
    return dict(inputs=inputs, targets=targets, active=active, lengths=lengths, b_values=b_values, c_values=c_values, step_sizes=step_sizes, decay_rates=decay_rates, in_weight=in_weight, out_weight=out_weight)


HIGH = lax.Precision.HIGHEST

def span_state(chan, bmat, steps, rates):
    heads = chan.shape[1]
    per = heads // bmat.shape[1]
    cumul = jnp.cumsum(-steps * rates[:, None], axis=1)
    scaled = chan * jnp.transpose(steps)[:, :, None]
    b_heads = jnp.repeat(bmat, per, axis=1)
    tail = jnp.exp(cumul[:, -1:] - cumul)
    fresh = jnp.einsum('shn,shp->hnp', b_heads * jnp.transpose(tail)[:, :, None], scaled, precision=HIGH)
    return (jnp.exp(cumul[:, -1]), fresh)

def span_forward(chan, bmat, cmat, steps, rates, state):
    heads = chan.shape[1]
    per = heads // bmat.shape[1]
    length = chan.shape[0]
    cumul = jnp.cumsum(-steps * rates[:, None], axis=1)
    scaled = chan * jnp.transpose(steps)[:, :, None]
    c_heads = jnp.repeat(cmat, per, axis=1)
    causal = (jnp.arange(length)[:, None] >= jnp.arange(length)[None, :])[None]
    spread = cumul[:, :, None] - cumul[:, None, :]
    weight = jnp.where(causal, jnp.exp(jnp.where(causal, spread, 0.0)), 0.0)
    scores = jnp.einsum('tgn,sgn->gts', cmat, bmat, precision=HIGH)
    scores = jnp.repeat(scores, per, axis=0) * weight
    inner = jnp.einsum('hts,shp->thp', scores, scaled, precision=HIGH)
    carried = jnp.einsum('thn,hnp->thp', c_heads, state, precision=HIGH)
    carried = carried * jnp.transpose(jnp.exp(cumul))[:, :, None]
    total, fresh = span_state(chan, bmat, steps, rates)
    return (inner + carried, total[:, None, None] * state + fresh)

def reference(inputs, targets, active, lengths, b_values, c_values, step_sizes, decay_rates, in_weight, out_weight):
    blocks = LENGTH // TOK_DEV
    grads_in, grads_b, grads_c, grads_s = ([], [], [], [])
    rate_total = jnp.zeros((HEADS,), jnp.float32)
    for index in range(TRANSCRIPTS):
        chan = jnp.dot(inputs[index], in_weight, preferred_element_type=jnp.float32).astype(jnp.bfloat16)
        live = (jnp.arange(LENGTH) < lengths[index]) & (active[index] == 1)
        cotan = jnp.where(live[:, None], -targets[index], jnp.zeros_like(targets[index]))
        dy_vals = jnp.dot(cotan, out_weight.T, preferred_element_type=jnp.float32).astype(jnp.bfloat16)
        chan4 = chan.astype(jnp.float32).reshape(LENGTH, HEADS, HEAD_SIZE)
        bmat = b_values[index].astype(jnp.float32).reshape(LENGTH, HEAD_GROUPS, STATE)
        cmat = c_values[index].astype(jnp.float32).reshape(LENGTH, HEAD_GROUPS, STATE)

        def whole(chan4, bmat, cmat, steps, rates):
            xs = chan4.reshape(blocks, TOK_DEV, HEADS, HEAD_SIZE)
            bs = bmat.reshape(blocks, TOK_DEV, HEAD_GROUPS, STATE)
            cs = cmat.reshape(blocks, TOK_DEV, HEAD_GROUPS, STATE)
            ss = jnp.transpose(steps.reshape(HEADS, blocks, TOK_DEV), (1, 0, 2))

            def advance(state, items):
                out, new_state = span_forward(items[0], items[1], items[2], items[3], rates, state)
                return (new_state, out)
            start = jnp.zeros((HEADS, STATE, HEAD_SIZE), jnp.float32)
            _, outs = lax.scan(advance, start, (xs, bs, cs, ss))
            return outs.reshape(LENGTH, HEADS, HEAD_SIZE)
        _, pullback = jax.vjp(whole, chan4, bmat, cmat, step_sizes[index], decay_rates)
        dchan, dbm, dcm, dsteps, drates = pullback(dy_vals.astype(jnp.float32).reshape(LENGTH, HEADS, HEAD_SIZE))
        dchan_b = dchan.reshape(LENGTH, HEADS * HEAD_SIZE).astype(jnp.bfloat16)
        grads_in.append(jnp.dot(dchan_b, in_weight.T, preferred_element_type=jnp.float32).astype(jnp.bfloat16))
        grads_b.append(dbm.reshape(LENGTH, HEAD_GROUPS * STATE))
        grads_c.append(dcm.reshape(LENGTH, HEAD_GROUPS * STATE))
        grads_s.append(dsteps)
        rate_total = rate_total + drates
    return (jnp.stack(grads_in), jnp.stack(grads_b), jnp.stack(grads_c), jnp.stack(grads_s), rate_total)
```

```python
import functools

import jax
import jax.numpy as jnp
from jax import lax
from jax.experimental import pallas as pl
from jax.experimental.pallas import tpu as pltpu
from jax.sharding import PartitionSpec as P

STATE = 128
CHUNK = 128
HIGH = lax.Precision.HIGHEST
F32 = jnp.float32
BF16 = jnp.bfloat16


def mm(a, b, ca=1, cb=0, precision=None):
    return lax.dot_general(
        a, b, (((ca,), (cb,)), ((), ())), preferred_element_type=F32, precision=precision
    )


def head_marks(per, size):
    row = lax.broadcasted_iota(jnp.int32, (per, per * size), 0)
    col = lax.broadcasted_iota(jnp.int32, (per, per * size), 1)
    return (col >= row * size) & (col < row * size + size)


def spread_heads(vals, marks):
    high = vals.astype(BF16)
    low = (vals - high.astype(F32)).astype(BF16)
    return mm(high, marks) + mm(low, marks)


def state_kernel(mat_ref, vals_ref, weight_ref, out_ref, *, per, size):
    marks = head_marks(per, size).astype(F32).astype(BF16)
    scaled = (vals_ref[...].astype(F32) * spread_heads(weight_ref[0], marks)).astype(BF16)
    out_ref[...] = mm(mat_ref[...], scaled, 0, 0)


def inner_kernel(
    x_ref, dy_ref, b_ref, c_ref, cum_ref, off_ref, dx_ref, db_ref, dc_ref, dlog_ref, col_ref, *, per, size
):
    tokens = x_ref.shape[0]
    row = lax.broadcasted_iota(jnp.int32, (CHUNK, CHUNK), 0)
    col = lax.broadcasted_iota(jnp.int32, (CHUNK, CHUNK), 1)
    causal = row <= col
    after = (row >= col).astype(F32)
    ones = jnp.ones((8, CHUNK), BF16)
    head = lax.broadcasted_iota(jnp.int32, (per, CHUNK), 0)

    for chunk in range(tokens // CHUNK):
        at = slice(chunk * CHUNK, (chunk + 1) * CHUNK)
        b = b_ref[at, :]
        c = c_ref[at, :]
        scores = jnp.where(causal, mm(b, c, 1, 1), 0.0)
        dscores = jnp.zeros((CHUNK, CHUNK), F32)
        rows = jnp.zeros((per, CHUNK), F32)
        cols = jnp.zeros((per, CHUNK), F32)
        for h in range(per):
            lanes = slice(h * size, (h + 1) * size)
            x = x_ref[at, lanes]
            dy = dy_ref[at, lanes]
            power = cum_ref[h : h + 1, at] + off_ref[0, at, h : h + 1]
            decay = jnp.exp(jnp.where(causal, power, 0.0))
            weight = scores * decay
            pair = mm(x, dy, 1, 1)
            dscores = dscores + pair * decay
            dx_ref[at, lanes] = mm(weight.astype(BF16), dy)
            terms = (pair * weight).astype(BF16)
            rows = jnp.where(head == h, mm(ones, terms)[:1, :], rows)
            cols = jnp.where(head == h, mm(ones, terms, 1, 1)[:1, :], cols)
        dscores = jnp.where(causal, dscores, 0.0).astype(BF16)
        db_ref[at, :] = mm(dscores, c)
        dc_ref[at, :] = mm(dscores, b, 0, 0)
        dlog_ref[:, at] = mm(rows - cols, after, precision=HIGH)
        col_ref[:, at] = cols


def outer_kernel(
    x_ref, dy_ref, b_ref, c_ref, tail_ref, grow_ref, growr_ref, step_ref, rate_ref,
    state_ref, grad_ref, dxi_ref, dbi_ref, dci_ref, dlogi_ref, coli_ref,
    dx_ref, db_ref, dc_ref, ds_ref, dr_ref, states, *, per, size,
):
    tokens = x_ref.shape[0]
    chunks = tokens // CHUNK
    row = lax.broadcasted_iota(jnp.int32, (CHUNK, CHUNK), 0)
    col = lax.broadcasted_iota(jnp.int32, (CHUNK, CHUNK), 1)
    after = (row >= col).astype(F32)
    before = (row < col).astype(F32)
    keep = head_marks(per, size)
    marks = keep.astype(F32).astype(BF16)
    rates = rate_ref[...]

    state = state_ref[...].astype(F32)
    for chunk in range(chunks):
        at = slice(chunk * CHUNK, (chunk + 1) * CHUNK)
        states[chunk] = state
        if chunk < chunks - 1:
            wx = (x_ref[at, :].astype(F32) * spread_heads(tail_ref[0, at, :], marks)).astype(BF16)
            total = spread_heads(grow_ref[0, (chunk + 1) * CHUNK - 8 : (chunk + 1) * CHUNK, :], marks)
            state = state * total[7:8, :] + mm(b_ref[at, :], wx, 0, 0)

    grad = grad_ref[...].astype(F32)
    rate_sum = jnp.zeros((per, 1), F32)
    for chunk in reversed(range(chunks)):
        at = slice(chunk * CHUNK, (chunk + 1) * CHUNK)
        b = b_ref[at, :]
        c = c_ref[at, :]
        x = x_ref[at, :].astype(F32)
        tail = spread_heads(tail_ref[0, at, :], marks)
        grow = spread_heads(grow_ref[0, at, :], marks)
        wx = (x * tail).astype(BF16)
        ey = dy_ref[at, :].astype(F32) * grow
        eyb = ey.astype(BF16)
        state = states[chunk]
        stateb = state.astype(BF16)
        gradb = grad.astype(BF16)
        carried = tail * mm(b, gradb)
        dx_ref[at, :] = (dxi_ref[at, :] + carried).astype(BF16)
        cols = mm(marks, (x * carried).astype(BF16), 1, 1)
        rows = mm(marks, (ey * mm(c, stateb)).astype(BF16), 1, 1)
        dc_ref[at, :] = dci_ref[at, :] + mm(eyb, stateb, 1, 1)
        db_ref[at, :] = dbi_ref[at, :] + mm(wx, gradb, 1, 1)
        both = jnp.sum(state * grad, axis=0, keepdims=True)
        both = jnp.sum(jnp.where(keep, both, 0.0), axis=1, keepdims=True)
        total = growr_ref[:, (chunk + 1) * CHUNK - 1 : (chunk + 1) * CHUNK]
        dlog = (
            dlogi_ref[:, at]
            + mm(rows, after, precision=HIGH)
            + mm(cols, before, precision=HIGH)
            + total * both
        )
        steps = step_ref[:, at]
        ds_ref[:, at] = (coli_ref[:, at] + cols) / steps - rates * dlog
        rate_sum = rate_sum - jnp.sum(steps * dlog, axis=1, keepdims=True)
        if chunk:
            grad = grad * grow[CHUNK - 1 :, :] + mm(c, eyb, 0, 0)
    dr_ref[...] = jnp.broadcast_to(rate_sum, dr_ref.shape)


def params():
    return pltpu.CompilerParams(vmem_limit_bytes=48 * 1024 * 1024)


def local(
    inputs, targets, active, lengths, b_values, c_values, step_sizes, decay_rates, in_weight, out_weight
):
    tokens = inputs.shape[1]
    width = in_weight.shape[1]
    heads = step_sizes.shape[1]
    size = width // heads
    groups = b_values.shape[2] // STATE
    per = heads // groups
    wide = per * size
    chunks = tokens // CHUNK
    split = lax.axis_size("tensor")
    spans = lax.axis_size("seq")

    position = lax.axis_index("seq") * tokens + jnp.arange(tokens)
    live = (position < lengths[0]) & (active[0] == 1)
    cotan = jnp.where(live[:, None], -targets[0], jnp.zeros_like(targets[0]))
    mine = lax.axis_index("tensor")

    steps = step_sizes[0]
    logs = (-steps * decay_rates[:, None]).reshape(heads, chunks, CHUNK)
    upto = (jnp.arange(CHUNK)[:, None] <= jnp.arange(CHUNK)[None, :]).astype(F32)
    cum3 = jnp.einsum("hct,ts->hcs", logs, upto, precision=HIGH)
    ends = cum3[:, :, -1]
    starts = [jnp.zeros((heads,), F32)]
    for i in range(chunks):
        starts.append(starts[-1] + ends[:, i])
    span3 = cum3 + jnp.stack(starts[:chunks], axis=1)[:, :, None]
    span_end = starts[chunks]
    steps3 = steps.reshape(heads, chunks, CHUNK)

    def columns(value):
        return jnp.transpose(value.reshape(groups, per, tokens), (0, 2, 1))

    cum = cum3.reshape(heads, tokens)
    growr = jnp.exp(cum)
    off = columns(jnp.log(steps3) - cum3)
    tail = columns(jnp.exp(ends[:, :, None] - cum3) * steps3)
    grow = columns(growr)
    span_tail = columns(jnp.exp(span_end[:, None, None] - span3) * steps3)
    span_grow = columns(jnp.exp(span3))
    total = jnp.repeat(jnp.exp(span_end), size)[None, :]

    if split == 2:
        half = inputs.shape[2]
        swap = [(0, 1), (1, 0)]
        other_in = lax.ppermute(inputs[0], "tensor", swap)
        other_cot = lax.ppermute(cotan, "tensor", swap)
        first = mm(inputs[0], lax.dynamic_slice_in_dim(in_weight, mine * half, half, 0))
        second = mm(cotan, lax.dynamic_slice_in_dim(out_weight, mine * half, half, 1), 1, 1)
        first = first + mm(other_in, lax.dynamic_slice_in_dim(in_weight, (1 - mine) * half, half, 0))
        second = second + mm(
            other_cot, lax.dynamic_slice_in_dim(out_weight, (1 - mine) * half, half, 1), 1, 1
        )
    else:
        first = mm(lax.all_gather(inputs[0], "tensor", axis=1, tiled=True), in_weight)
        second = mm(lax.all_gather(cotan, "tensor", axis=1, tiled=True), out_weight, 1, 1)
    x = first.astype(BF16)
    dy = second.astype(BF16)
    bmat = b_values[0]
    cmat = c_values[0]

    values = pl.BlockSpec((tokens, wide), lambda g: (0, g))
    maps = pl.BlockSpec((tokens, STATE), lambda g: (0, g))
    rows = pl.BlockSpec((per, tokens), lambda g: (g, 0))
    cols = pl.BlockSpec((1, tokens, per), lambda g: (g, 0, 0))
    state = pl.BlockSpec((STATE, wide), lambda g: (0, g))
    f32 = functools.partial(jax.ShapeDtypeStruct, dtype=F32)

    def states_of(mat, vals, weight):
        return pl.pallas_call(
            functools.partial(state_kernel, per=per, size=size),
            grid=(groups,),
            in_specs=[maps, values, cols],
            out_specs=state,
            out_shape=f32((STATE, width)),
            compiler_params=params(),
            cost_estimate=pl.CostEstimate(
                flops=2 * tokens * STATE * width, bytes_accessed=4 * tokens * width, transcendentals=0
            ),
        )(mat, vals, weight)

    fresh = states_of(bmat, x, span_tail)
    pull = states_of(cmat, dy, span_grow)

    def along(own, by):
        pairs = [(i, i + by) for i in range(spans) if 0 <= i + by < spans]
        carry = lax.ppermute(own.astype(BF16), "seq", pairs)
        for _ in range(spans - 2):
            carry = lax.ppermute((total * carry.astype(F32) + own).astype(BF16), "seq", pairs)
        return carry

    if spans > 1:
        state_in = along(fresh, 1)
        grad_out = along(pull, -1)
    else:
        state_in = jnp.zeros_like(fresh)
        grad_out = jnp.zeros_like(pull)

    dxi, dbi, dci, dlogi, coli = pl.pallas_call(
        functools.partial(inner_kernel, per=per, size=size),
        grid=(groups,),
        in_specs=[values, values, maps, maps, rows, cols],
        out_specs=[values, maps, maps, rows, rows],
        out_shape=[
            f32((tokens, width)), f32((tokens, groups * STATE)), f32((tokens, groups * STATE)),
            f32((heads, tokens)), f32((heads, tokens)),
        ],
        compiler_params=params(),
        cost_estimate=pl.CostEstimate(
            flops=20000000000, bytes_accessed=8 * tokens * width, transcendentals=0
        ),
    )(x, dy, bmat, cmat, cum, off)

    dchan, grad_b, grad_c, dsteps, drates = pl.pallas_call(
        functools.partial(outer_kernel, per=per, size=size),
        grid=(groups,),
        in_specs=[
            values, values, maps, maps, cols, cols, rows, rows,
            pl.BlockSpec((per, 1), lambda g: (g, 0)),
            state, state, values, maps, maps, rows, rows,
        ],
        out_specs=[values, maps, maps, rows, pl.BlockSpec((per, 128), lambda g: (g, 0))],
        out_shape=[
            jax.ShapeDtypeStruct((tokens, width), BF16),
            f32((tokens, groups * STATE)), f32((tokens, groups * STATE)),
            f32((heads, tokens)), f32((heads, 128)),
        ],
        scratch_shapes=[pltpu.VMEM((chunks, STATE, wide), F32)],
        compiler_params=params(),
    )(
        x, dy, bmat, cmat, tail, grow, growr, steps, decay_rates[:, None],
        state_in, grad_out, dxi, dbi, dci, dlogi, coli,
    )

    if split == 2:
        theirs = mm(dchan, lax.dynamic_slice_in_dim(in_weight, (1 - mine) * half, half, 0), 1, 1)
        arrived = lax.ppermute(theirs.astype(BF16), "tensor", swap)
        own = mm(dchan, lax.dynamic_slice_in_dim(in_weight, mine * half, half, 0), 1, 1)
        grad_inputs = (own + arrived.astype(F32)).astype(BF16)[None]
    else:
        grad_inputs = lax.psum_scatter(
            mm(dchan, in_weight, 1, 1), "tensor", scatter_dimension=1, tiled=True
        ).astype(BF16)[None]
    rate_total = lax.psum(drates[:, 0], ("seq", "dp"))
    return (grad_inputs, grad_b[None], grad_c[None], dsteps[None], rate_total)


def solution(mesh):
    in_specs = (
        P(("groups", "dp"), "seq", "tensor"),
        P(("groups", "dp"), "seq", "tensor"),
        P(("groups", "dp"), "seq"),
        P(("groups", "dp")),
        P(("groups", "dp"), "seq", "tensor"),
        P(("groups", "dp"), "seq", "tensor"),
        P(("groups", "dp"), "tensor", "seq"),
        P("tensor"),
        P(None, "tensor"),
        P("tensor", None),
    )
    out_specs = (
        P(("groups", "dp"), "seq", "tensor"),
        P(("groups", "dp"), "seq", "tensor"),
        P(("groups", "dp"), "seq", "tensor"),
        P(("groups", "dp"), "tensor", "seq"),
        P(("groups", "tensor")),
    )
    return jax.shard_map(local, mesh=mesh, in_specs=in_specs, out_specs=out_specs, check_vma=False)
```

```python
import functools

import jax
import jax.numpy as jnp
from jax import lax
from jax.experimental import pallas as pl
from jax.experimental.pallas import tpu as pltpu
from jax.sharding import PartitionSpec as P

STATE = 128
CHUNK = 128
HIGH = lax.Precision.HIGHEST
F32 = jnp.float32
BF16 = jnp.bfloat16


def mm(a, b, ca=1, cb=0, precision=None):
    return lax.dot_general(
        a, b, (((ca,), (cb,)), ((), ())), preferred_element_type=F32, precision=precision
    )


def head_marks(per, size):
    row = lax.broadcasted_iota(jnp.int32, (per, per * size), 0)
    col = lax.broadcasted_iota(jnp.int32, (per, per * size), 1)
    return (col >= row * size) & (col < row * size + size)


def spread_heads(vals, marks):
    high = vals.astype(BF16)
    low = (vals - high.astype(F32)).astype(BF16)
    return mm(high, marks) + mm(low, marks)


def state_kernel(mat_ref, vals_ref, weight_ref, out_ref, *, per, size):
    marks = head_marks(per, size).astype(F32).astype(BF16)
    scaled = (vals_ref[...].astype(F32) * spread_heads(weight_ref[0], marks)).astype(BF16)
    out_ref[...] = mm(mat_ref[...], scaled, 0, 0)


def inner_kernel(
    x_ref, dy_ref, b_ref, c_ref, cum_ref, off_ref, _one, _two,
    dx_ref, db_ref, dc_ref, dlog_ref, col_ref, *, per, size,
):
    tokens = x_ref.shape[0]
    row = lax.broadcasted_iota(jnp.int32, (CHUNK, CHUNK), 0)
    col = lax.broadcasted_iota(jnp.int32, (CHUNK, CHUNK), 1)
    causal = row <= col
    after = (row >= col).astype(F32)
    ones = jnp.ones((8, CHUNK), BF16)
    head = lax.broadcasted_iota(jnp.int32, (per, CHUNK), 0)

    for chunk in range(tokens // CHUNK):
        at = slice(chunk * CHUNK, (chunk + 1) * CHUNK)
        b = b_ref[at, :]
        c = c_ref[at, :]
        scores = jnp.where(causal, mm(b, c, 1, 1), 0.0)
        dscores = jnp.zeros((CHUNK, CHUNK), F32)
        rows = jnp.zeros((per, CHUNK), F32)
        cols = jnp.zeros((per, CHUNK), F32)
        for h in range(per):
            lanes = slice(h * size, (h + 1) * size)
            x = x_ref[at, lanes]
            dy = dy_ref[at, lanes]
            power = cum_ref[h : h + 1, at] + off_ref[0, at, h : h + 1]
            decay = jnp.exp(jnp.where(causal, power, 0.0))
            weight = scores * decay
            pair = mm(x, dy, 1, 1)
            dscores = dscores + pair * decay
            dx_ref[at, lanes] = mm(weight.astype(BF16), dy)
            terms = (pair * weight).astype(BF16)
            rows = jnp.where(head == h, mm(ones, terms)[:1, :], rows)
            cols = jnp.where(head == h, mm(ones, terms, 1, 1)[:1, :], cols)
        dscores = jnp.where(causal, dscores, 0.0).astype(BF16)
        db_ref[at, :] = mm(dscores, c)
        dc_ref[at, :] = mm(dscores, b, 0, 0)
        dlog_ref[:, at] = mm(rows - cols, after, precision=HIGH)
        col_ref[:, at] = cols


def step_kernel(total_ref, one_ref, fresh_ref, two_ref, pull_ref, _dep, first_ref, second_ref):
    total = total_ref[...]
    first_ref[...] = (total * one_ref[...].astype(F32) + fresh_ref[...]).astype(BF16)
    second_ref[...] = (total * two_ref[...].astype(F32) + pull_ref[...]).astype(BF16)


def outer_kernel(
    x_ref, dy_ref, b_ref, c_ref, tail_ref, grow_ref, growr_ref, step_ref, rate_ref,
    state_ref, grad_ref, dxi_ref, dbi_ref, dci_ref, dlogi_ref, coli_ref, *rest, first, last, per, size,
):
    dx_ref, db_ref, dc_ref, ds_ref, dr_ref, out_ref, states = rest[-7:]
    row = lax.broadcasted_iota(jnp.int32, (CHUNK, CHUNK), 0)
    col = lax.broadcasted_iota(jnp.int32, (CHUNK, CHUNK), 1)
    after = (row >= col).astype(F32)
    before = (row < col).astype(F32)
    keep = head_marks(per, size)
    marks = keep.astype(F32).astype(BF16)
    rates = rate_ref[...]

    state = state_ref[...].astype(F32)
    for chunk in range(last):
        at = slice(chunk * CHUNK, (chunk + 1) * CHUNK)
        states[chunk] = state
        if chunk < last - 1:
            wx = (x_ref[at, :].astype(F32) * spread_heads(tail_ref[0, at, :], marks)).astype(BF16)
            total = spread_heads(grow_ref[0, (chunk + 1) * CHUNK - 8 : (chunk + 1) * CHUNK, :], marks)
            state = state * total[7:8, :] + mm(b_ref[at, :], wx, 0, 0)

    grad = grad_ref[...].astype(F32)
    rate_sum = jnp.zeros((per, 1), F32)
    for chunk in reversed(range(first, last)):
        at = slice(chunk * CHUNK, (chunk + 1) * CHUNK)
        to = slice((chunk - first) * CHUNK, (chunk - first + 1) * CHUNK)
        b = b_ref[at, :]
        c = c_ref[at, :]
        x = x_ref[at, :].astype(F32)
        tail = spread_heads(tail_ref[0, at, :], marks)
        grow = spread_heads(grow_ref[0, at, :], marks)
        wx = (x * tail).astype(BF16)
        ey = dy_ref[at, :].astype(F32) * grow
        eyb = ey.astype(BF16)
        state = states[chunk]
        stateb = state.astype(BF16)
        gradb = grad.astype(BF16)
        carried = tail * mm(b, gradb)
        dx_ref[to, :] = (dxi_ref[to, :] + carried).astype(BF16)
        cols = mm(marks, (x * carried).astype(BF16), 1, 1)
        rows = mm(marks, (ey * mm(c, stateb)).astype(BF16), 1, 1)
        dc_ref[to, :] = dci_ref[to, :] + mm(eyb, stateb, 1, 1)
        db_ref[to, :] = dbi_ref[to, :] + mm(wx, gradb, 1, 1)
        both = jnp.sum(state * grad, axis=0, keepdims=True)
        both = jnp.sum(jnp.where(keep, both, 0.0), axis=1, keepdims=True)
        total = growr_ref[:, (chunk + 1) * CHUNK - 1 : (chunk + 1) * CHUNK]
        dlog = (
            dlogi_ref[:, to]
            + mm(rows, after, precision=HIGH)
            + mm(cols, before, precision=HIGH)
            + total * both
        )
        steps = step_ref[:, at]
        ds_ref[:, to] = (coli_ref[:, to] + cols) / steps - rates * dlog
        rate_sum = rate_sum - jnp.sum(steps * dlog, axis=1, keepdims=True)
        grad = grad * grow[CHUNK - 1 :, :] + mm(c, eyb, 0, 0)
    dr_ref[...] = jnp.broadcast_to(rate_sum, dr_ref.shape)
    out_ref[...] = grad


def params():
    return pltpu.CompilerParams(vmem_limit_bytes=48 * 1024 * 1024)


def local(
    inputs, targets, active, lengths, b_values, c_values, step_sizes, decay_rates, in_weight, out_weight
):
    tokens = inputs.shape[1]
    width = in_weight.shape[1]
    heads = step_sizes.shape[1]
    size = width // heads
    groups = b_values.shape[2] // STATE
    per = heads // groups
    wide = per * size
    chunks = tokens // CHUNK
    split = lax.axis_size("tensor")
    spans = lax.axis_size("seq")

    position = lax.axis_index("seq") * tokens + jnp.arange(tokens)
    live = (position < lengths[0]) & (active[0] == 1)
    cotan = jnp.where(live[:, None], -targets[0], jnp.zeros_like(targets[0]))
    mine = lax.axis_index("tensor")

    steps = step_sizes[0]
    logs = (-steps * decay_rates[:, None]).reshape(heads, chunks, CHUNK)
    upto = (jnp.arange(CHUNK)[:, None] <= jnp.arange(CHUNK)[None, :]).astype(F32)
    cum3 = jnp.einsum("hct,ts->hcs", logs, upto, precision=HIGH)
    ends = cum3[:, :, -1]
    starts = [jnp.zeros((heads,), F32)]
    for i in range(chunks):
        starts.append(starts[-1] + ends[:, i])
    span3 = cum3 + jnp.stack(starts[:chunks], axis=1)[:, :, None]
    span_end = starts[chunks]
    steps3 = steps.reshape(heads, chunks, CHUNK)

    def columns(value):
        return jnp.transpose(value.reshape(groups, per, tokens), (0, 2, 1))

    cum = cum3.reshape(heads, tokens)
    growr = jnp.exp(cum)
    off = columns(jnp.log(steps3) - cum3)
    tail = columns(jnp.exp(ends[:, :, None] - cum3) * steps3)
    grow = columns(growr)
    span_tail = columns(jnp.exp(span_end[:, None, None] - span3) * steps3)
    span_grow = columns(jnp.exp(span3))
    total = jnp.repeat(jnp.exp(span_end), size)[None, :]

    if split == 2:
        half = inputs.shape[2]
        swap = [(0, 1), (1, 0)]
        other_in = lax.ppermute(inputs[0], "tensor", swap)
        other_cot = lax.ppermute(cotan, "tensor", swap)
        first = mm(inputs[0], lax.dynamic_slice_in_dim(in_weight, mine * half, half, 0))
        second = mm(cotan, lax.dynamic_slice_in_dim(out_weight, mine * half, half, 1), 1, 1)
        first = first + mm(other_in, lax.dynamic_slice_in_dim(in_weight, (1 - mine) * half, half, 0))
        second = second + mm(
            other_cot, lax.dynamic_slice_in_dim(out_weight, (1 - mine) * half, half, 1), 1, 1
        )
    else:
        first = mm(lax.all_gather(inputs[0], "tensor", axis=1, tiled=True), in_weight)
        second = mm(lax.all_gather(cotan, "tensor", axis=1, tiled=True), out_weight, 1, 1)
    x = first.astype(BF16)
    dy = second.astype(BF16)
    bmat = b_values[0]
    cmat = c_values[0]

    values = pl.BlockSpec((tokens, wide), lambda g: (0, g))
    maps = pl.BlockSpec((tokens, STATE), lambda g: (0, g))
    rows = pl.BlockSpec((per, tokens), lambda g: (g, 0))
    cols = pl.BlockSpec((1, tokens, per), lambda g: (g, 0, 0))
    state = pl.BlockSpec((STATE, wide), lambda g: (0, g))
    f32 = functools.partial(jax.ShapeDtypeStruct, dtype=F32)

    def states_of(mat, vals, weight):
        return pl.pallas_call(
            functools.partial(state_kernel, per=per, size=size),
            grid=(groups,),
            in_specs=[maps, values, cols],
            out_specs=state,
            out_shape=f32((STATE, width)),
            compiler_params=params(),
            cost_estimate=pl.CostEstimate(
                flops=2 * tokens * STATE * width, bytes_accessed=4 * tokens * width, transcendentals=0
            ),
        )(mat, vals, weight)

    fresh = states_of(bmat, x, span_tail)
    pull = states_of(cmat, dy, span_grow)

    half_tokens = tokens // 2
    anywhere = pl.BlockSpec(memory_space=pl.ANY)

    def inner(part, one, two):
        part_values = pl.BlockSpec((half_tokens, wide), lambda g: (part, g))
        part_maps = pl.BlockSpec((half_tokens, STATE), lambda g: (part, g))
        new_values = pl.BlockSpec((half_tokens, wide), lambda g: (0, g))
        new_maps = pl.BlockSpec((half_tokens, STATE), lambda g: (0, g))
        new_rows = pl.BlockSpec((per, half_tokens), lambda g: (g, 0))
        return pl.pallas_call(
            functools.partial(inner_kernel, per=per, size=size),
            grid=(groups,),
            in_specs=[
                part_values, part_values, part_maps, part_maps,
                pl.BlockSpec((per, half_tokens), lambda g: (g, part)),
                pl.BlockSpec((1, half_tokens, per), lambda g: (g, part, 0)),
                anywhere, anywhere,
            ],
            out_specs=[new_values, new_maps, new_maps, new_rows, new_rows],
            out_shape=[
                f32((half_tokens, width)), f32((half_tokens, groups * STATE)),
                f32((half_tokens, groups * STATE)), f32((heads, half_tokens)), f32((heads, half_tokens)),
            ],
            compiler_params=params(),
            cost_estimate=pl.CostEstimate(
                flops=10000000000, bytes_accessed=4 * tokens * width, transcendentals=0
            ),
        )(x, dy, bmat, cmat, cum, off, one, two)

    def advance(one, two, dep):
        return pl.pallas_call(
            step_kernel,
            grid=(groups,),
            in_specs=[pl.BlockSpec((1, wide), lambda g: (0, g)), state, state, state, state, anywhere],
            out_specs=[state, state],
            out_shape=[jax.ShapeDtypeStruct((STATE, width), BF16)] * 2,
            compiler_params=params(),
        )(total, one, fresh, two, pull, dep)

    def hop(value, by):
        pairs = [(i, i + by) for i in range(spans) if 0 <= i + by < spans]
        return lax.ppermute(value, "seq", pairs)

    parts = [None, None]
    if spans > 3:
        back = hop(pull.astype(BF16), -1)
        to_prev = (total * back.astype(F32) + pull).astype(BF16)
        to_next = fresh.astype(BF16)
        back = hop(to_prev, -1)
        ahead = hop(to_next, 1)
        parts[1] = inner(1, to_next, to_prev)
        to_next, to_prev = advance(ahead, back, parts[1][3])
        back = hop(to_prev, -1)
        ahead = hop(to_next, 1)
        parts[0] = inner(0, to_next, to_prev)
        to_next, to_prev = advance(ahead, back, parts[0][3])
        ahead = hop(to_next, 1)
        for _ in range(spans - 4):
            ahead = hop((total * ahead.astype(F32) + fresh).astype(BF16), 1)
            back = hop((total * back.astype(F32) + pull).astype(BF16), -1)
    else:
        ahead = jnp.zeros((STATE, width), BF16)
        back = ahead
        for _ in range(spans - 1):
            ahead = hop((total * ahead.astype(F32) + fresh).astype(BF16), 1)
            back = hop((total * back.astype(F32) + pull).astype(BF16), -1)
        parts = [inner(0, x, x), inner(1, x, x)]

    def outer(part, grad, deps):
        new_values = pl.BlockSpec((half_tokens, wide), lambda g: (0, g))
        new_maps = pl.BlockSpec((half_tokens, STATE), lambda g: (0, g))
        new_rows = pl.BlockSpec((per, half_tokens), lambda g: (g, 0))
        part_maps = pl.BlockSpec((half_tokens, STATE), lambda g: (part, g))
        in_specs = [
            values, values, maps, maps, cols, cols, rows, rows,
            pl.BlockSpec((per, 1), lambda g: (g, 0)),
            state, state, new_values, new_maps, new_maps, new_rows, new_rows,
        ] + [anywhere] * len(deps)
        return pl.pallas_call(
            functools.partial(
                outer_kernel, first=part * chunks // 2, last=(part + 1) * chunks // 2, per=per, size=size
            ),
            grid=(groups,),
            in_specs=in_specs,
            out_specs=[
                new_values, part_maps, part_maps,
                pl.BlockSpec((per, half_tokens), lambda g: (g, part)),
                pl.BlockSpec((per, 128), lambda g: (g, 0)), state,
            ],
            out_shape=[
                jax.ShapeDtypeStruct((half_tokens, width), BF16),
                f32((tokens, groups * STATE)), f32((tokens, groups * STATE)),
                f32((heads, tokens)), f32((heads, 128)), f32((STATE, width)),
            ],
            scratch_shapes=[pltpu.VMEM((chunks, STATE, wide), F32)],
            compiler_params=params(),
            input_output_aliases={16: 1, 17: 2, 18: 3} if deps else {},
            cost_estimate=pl.CostEstimate(
                flops=6000000000, bytes_accessed=8 * tokens * width, transcendentals=0
            ),
        )(
            x, dy, bmat, cmat, tail, grow, growr, steps, decay_rates[:, None], ahead, grad,
            *parts[part], *deps,
        )

    late, grad_b, grad_c, dsteps, late_rates, middle = outer(1, back, [])
    if split == 2:
        weight_own = lax.dynamic_slice_in_dim(in_weight, mine * half, half, 0)
        weight_other = lax.dynamic_slice_in_dim(in_weight, (1 - mine) * half, half, 0)
        late_send = mm(late, weight_other, 1, 1).astype(BF16)
        late_got = lax.ppermute(late_send, "tensor", swap)
    else:
        late_send = late
    early, grad_b, grad_c, dsteps, early_rates, _ = outer(0, middle, [grad_b, grad_c, dsteps, late_send])
    drates = late_rates + early_rates

    if split == 2:
        early_send = mm(early, weight_other, 1, 1).astype(BF16)
        early_got = lax.ppermute(early_send, "tensor", swap)
        late_own = mm(late, weight_own, 1, 1) + late_got.astype(F32)
        early_own = mm(early, weight_own, 1, 1)
        early_own, late_own = lax.optimization_barrier((early_own, late_own))
        grad_inputs = jnp.concatenate(
            [(early_own + early_got.astype(F32)).astype(BF16), late_own.astype(BF16)], axis=0
        )[None]
    else:
        grad_inputs = lax.psum_scatter(
            mm(jnp.concatenate([early, late], axis=0), in_weight, 1, 1), "tensor", scatter_dimension=1, tiled=True
        ).astype(BF16)[None]
    rate_total = lax.psum(drates[:, 0], ("seq", "dp"))
    return (grad_inputs, grad_b[None], grad_c[None], dsteps[None], rate_total)


def solution(mesh):
    in_specs = (
        P(("groups", "dp"), "seq", "tensor"),
        P(("groups", "dp"), "seq", "tensor"),
        P(("groups", "dp"), "seq"),
        P(("groups", "dp")),
        P(("groups", "dp"), "seq", "tensor"),
        P(("groups", "dp"), "seq", "tensor"),
        P(("groups", "dp"), "tensor", "seq"),
        P("tensor"),
        P(None, "tensor"),
        P("tensor", None),
    )
    out_specs = (
        P(("groups", "dp"), "seq", "tensor"),
        P(("groups", "dp"), "seq", "tensor"),
        P(("groups", "dp"), "seq", "tensor"),
        P(("groups", "dp"), "tensor", "seq"),
        P(("groups", "tensor")),
    )
    return jax.shard_map(local, mesh=mesh, in_specs=in_specs, out_specs=out_specs, check_vma=False)
```

```python
import functools

import jax
import jax.numpy as jnp
from jax import lax
from jax.experimental import pallas as pl
from jax.experimental.pallas import tpu as pltpu
from jax.sharding import PartitionSpec as P

STATE = 128
CHUNK = 128
HIGH = lax.Precision.HIGHEST
F32 = jnp.float32
BF16 = jnp.bfloat16


def mm(a, b, ca=1, cb=0, precision=None):
    return lax.dot_general(
        a, b, (((ca,), (cb,)), ((), ())), preferred_element_type=F32, precision=precision
    )


def head_marks(per, size):
    row = lax.broadcasted_iota(jnp.int32, (per, per * size), 0)
    col = lax.broadcasted_iota(jnp.int32, (per, per * size), 1)
    return (col >= row * size) & (col < row * size + size)


def spread_heads(vals, marks):
    high = vals.astype(BF16)
    low = (vals - high.astype(F32)).astype(BF16)
    return mm(high, marks) + mm(low, marks)


def state_kernel(mat_ref, vals_ref, weight_ref, out_ref, *, per, size):
    marks = head_marks(per, size).astype(F32).astype(BF16)
    scaled = (vals_ref[...].astype(F32) * spread_heads(weight_ref[0], marks)).astype(BF16)
    out_ref[...] = mm(mat_ref[...], scaled, 0, 0)


def inner_kernel(
    x_ref, dy_ref, b_ref, c_ref, cum_ref, off_ref, _one, _two,
    dx_ref, db_ref, dc_ref, dlog_ref, col_ref, *, per, size,
):
    tokens = x_ref.shape[0]
    row = lax.broadcasted_iota(jnp.int32, (CHUNK, CHUNK), 0)
    col = lax.broadcasted_iota(jnp.int32, (CHUNK, CHUNK), 1)
    causal = row <= col
    after = (row >= col).astype(F32)
    ones = jnp.ones((8, CHUNK), BF16)
    head = lax.broadcasted_iota(jnp.int32, (per, CHUNK), 0)
    marks = head_marks(per, CHUNK).astype(F32).astype(BF16)
    pack = 2
    pair_width = pack * size
    lane = lax.broadcasted_iota(jnp.int32, (CHUNK, pair_width), 1)
    left = (lane < size).astype(F32).astype(BF16)
    right = (lane >= size).astype(F32).astype(BF16)

    for chunk in range(tokens // CHUNK):
        at = slice(chunk * CHUNK, (chunk + 1) * CHUNK)
        b = b_ref[at, :]
        c = c_ref[at, :]
        scores = jnp.where(causal, mm(b, c, 1, 1), 0.0)
        dscores = jnp.zeros((CHUNK, CHUNK), F32)
        terms = []
        for j in range(per // pack):
            lanes = slice(j * pair_width, (j + 1) * pair_width)
            x = x_ref[at, lanes]
            dy = dy_ref[at, lanes]
            pairs = mm(jnp.concatenate([x * left, x * right], axis=0), dy, 1, 1)
            weights = []
            for k in range(pack):
                h = j * pack + k
                decay = jnp.exp(cum_ref[h : h + 1, at] + off_ref[0, at, h : h + 1])
                weight = scores * decay
                pair = pairs[k * CHUNK : (k + 1) * CHUNK, :]
                dscores = dscores + pair * decay
                weights.append(weight.astype(BF16))
                terms.append((pair * weight).astype(BF16))
            dx_ref[at, lanes] = mm(
                jnp.concatenate(weights, axis=1), jnp.concatenate([dy * left, dy * right], axis=0)
            )
        terms = jnp.concatenate(terms, axis=0)
        rows = mm(marks, terms)
        sums = mm(ones, terms, 1, 1)
        cols = jnp.zeros((per, CHUNK), F32)
        for h in range(per):
            cols = jnp.where(head == h, sums[:1, h * CHUNK : (h + 1) * CHUNK], cols)
        dscores = jnp.where(causal, dscores, 0.0).astype(BF16)
        db_ref[at, :] = mm(dscores, c)
        dc_ref[at, :] = mm(dscores, b, 0, 0)
        dlog_ref[:, at] = mm(rows - cols, after, precision=HIGH)
        col_ref[:, at] = cols


def step_kernel(total_ref, one_ref, fresh_ref, two_ref, pull_ref, _dep, first_ref, second_ref):
    total = total_ref[...]
    first_ref[...] = (total * one_ref[...].astype(F32) + fresh_ref[...]).astype(BF16)
    second_ref[...] = (total * two_ref[...].astype(F32) + pull_ref[...]).astype(BF16)


def outer_kernel(
    x_ref, dy_ref, b_ref, c_ref, tail_ref, grow_ref, growr_ref, step_ref, rate_ref,
    state_ref, grad_ref, dxi_ref, dbi_ref, dci_ref, dlogi_ref, coli_ref, *rest, first, last, per, size,
):
    dx_ref, db_ref, dc_ref, ds_ref, dr_ref, out_ref, states = rest[-7:]
    row = lax.broadcasted_iota(jnp.int32, (CHUNK, CHUNK), 0)
    col = lax.broadcasted_iota(jnp.int32, (CHUNK, CHUNK), 1)
    after = (row >= col).astype(F32)
    before = (row < col).astype(F32)
    keep = head_marks(per, size)
    marks = keep.astype(F32).astype(BF16)
    rates = rate_ref[...]

    state = state_ref[...].astype(F32)
    for chunk in range(last):
        at = slice(chunk * CHUNK, (chunk + 1) * CHUNK)
        states[chunk] = state
        if chunk < last - 1:
            wx = (x_ref[at, :].astype(F32) * spread_heads(tail_ref[0, at, :], marks)).astype(BF16)
            total = spread_heads(grow_ref[0, (chunk + 1) * CHUNK - 8 : (chunk + 1) * CHUNK, :], marks)
            state = state * total[7:8, :] + mm(b_ref[at, :], wx, 0, 0)

    grad = grad_ref[...].astype(F32)
    rate_sum = jnp.zeros((per, 1), F32)
    for chunk in reversed(range(first, last)):
        at = slice(chunk * CHUNK, (chunk + 1) * CHUNK)
        to = slice((chunk - first) * CHUNK, (chunk - first + 1) * CHUNK)
        b = b_ref[at, :]
        c = c_ref[at, :]
        x = x_ref[at, :].astype(F32)
        tail = spread_heads(tail_ref[0, at, :], marks)
        grow = spread_heads(grow_ref[0, at, :], marks)
        wx = (x * tail).astype(BF16)
        ey = dy_ref[at, :].astype(F32) * grow
        eyb = ey.astype(BF16)
        state = states[chunk]
        stateb = state.astype(BF16)
        gradb = grad.astype(BF16)
        carried = tail * mm(b, gradb)
        dx_ref[to, :] = (dxi_ref[to, :] + carried).astype(BF16)
        cols = mm(marks, (x * carried).astype(BF16), 1, 1)
        rows = mm(marks, (ey * mm(c, stateb)).astype(BF16), 1, 1)
        dc_ref[to, :] = dci_ref[to, :] + mm(eyb, stateb, 1, 1)
        db_ref[to, :] = dbi_ref[to, :] + mm(wx, gradb, 1, 1)
        both = jnp.sum(state * grad, axis=0, keepdims=True)
        both = jnp.sum(jnp.where(keep, both, 0.0), axis=1, keepdims=True)
        total = growr_ref[:, (chunk + 1) * CHUNK - 1 : (chunk + 1) * CHUNK]
        dlog = (
            dlogi_ref[:, to]
            + mm(rows, after, precision=HIGH)
            + mm(cols, before, precision=HIGH)
            + total * both
        )
        steps = step_ref[:, at]
        ds_ref[:, to] = (coli_ref[:, to] + cols) / steps - rates * dlog
        rate_sum = rate_sum - jnp.sum(steps * dlog, axis=1, keepdims=True)
        grad = grad * grow[CHUNK - 1 :, :] + mm(c, eyb, 0, 0)
    dr_ref[...] = jnp.broadcast_to(rate_sum, dr_ref.shape)
    out_ref[...] = grad


def params():
    return pltpu.CompilerParams(vmem_limit_bytes=48 * 1024 * 1024)


def local(
    inputs, targets, active, lengths, b_values, c_values, step_sizes, decay_rates, in_weight, out_weight
):
    tokens = inputs.shape[1]
    width = in_weight.shape[1]
    heads = step_sizes.shape[1]
    size = width // heads
    groups = b_values.shape[2] // STATE
    per = heads // groups
    wide = per * size
    chunks = tokens // CHUNK
    split = lax.axis_size("tensor")
    spans = lax.axis_size("seq")

    position = lax.axis_index("seq") * tokens + jnp.arange(tokens)
    live = (position < lengths[0]) & (active[0] == 1)
    cotan = jnp.where(live[:, None], -targets[0], jnp.zeros_like(targets[0]))
    mine = lax.axis_index("tensor")

    steps = step_sizes[0]
    logs = (-steps * decay_rates[:, None]).reshape(heads, chunks, CHUNK)
    upto = (jnp.arange(CHUNK)[:, None] <= jnp.arange(CHUNK)[None, :]).astype(F32)
    cum3 = jnp.einsum("hct,ts->hcs", logs, upto, precision=HIGH)
    ends = cum3[:, :, -1]
    starts = [jnp.zeros((heads,), F32)]
    for i in range(chunks):
        starts.append(starts[-1] + ends[:, i])
    span3 = cum3 + jnp.stack(starts[:chunks], axis=1)[:, :, None]
    span_end = starts[chunks]
    steps3 = steps.reshape(heads, chunks, CHUNK)

    def columns(value):
        return jnp.transpose(value.reshape(groups, per, tokens), (0, 2, 1))

    cum = cum3.reshape(heads, tokens)
    growr = jnp.exp(cum)
    off = columns(jnp.log(steps3) - cum3)
    tail = columns(jnp.exp(ends[:, :, None] - cum3) * steps3)
    grow = columns(growr)
    span_tail = columns(jnp.exp(span_end[:, None, None] - span3) * steps3)
    span_grow = columns(jnp.exp(span3))
    total = jnp.repeat(jnp.exp(span_end), size)[None, :]

    if split == 2:
        half = inputs.shape[2]
        swap = [(0, 1), (1, 0)]
        other_in = lax.ppermute(inputs[0], "tensor", swap)
        other_cot = lax.ppermute(cotan, "tensor", swap)
        first = mm(inputs[0], lax.dynamic_slice_in_dim(in_weight, mine * half, half, 0))
        second = mm(cotan, lax.dynamic_slice_in_dim(out_weight, mine * half, half, 1), 1, 1)
        first = first + mm(other_in, lax.dynamic_slice_in_dim(in_weight, (1 - mine) * half, half, 0))
        second = second + mm(
            other_cot, lax.dynamic_slice_in_dim(out_weight, (1 - mine) * half, half, 1), 1, 1
        )
    else:
        first = mm(lax.all_gather(inputs[0], "tensor", axis=1, tiled=True), in_weight)
        second = mm(lax.all_gather(cotan, "tensor", axis=1, tiled=True), out_weight, 1, 1)
    x = first.astype(BF16)
    dy = second.astype(BF16)
    bmat = b_values[0]
    cmat = c_values[0]

    values = pl.BlockSpec((tokens, wide), lambda g: (0, g))
    maps = pl.BlockSpec((tokens, STATE), lambda g: (0, g))
    rows = pl.BlockSpec((per, tokens), lambda g: (g, 0))
    cols = pl.BlockSpec((1, tokens, per), lambda g: (g, 0, 0))
    state = pl.BlockSpec((STATE, wide), lambda g: (0, g))
    f32 = functools.partial(jax.ShapeDtypeStruct, dtype=F32)

    def states_of(mat, vals, weight):
        return pl.pallas_call(
            functools.partial(state_kernel, per=per, size=size),
            grid=(groups,),
            in_specs=[maps, values, cols],
            out_specs=state,
            out_shape=f32((STATE, width)),
            compiler_params=params(),
            cost_estimate=pl.CostEstimate(
                flops=2 * tokens * STATE * width, bytes_accessed=4 * tokens * width, transcendentals=0
            ),
        )(mat, vals, weight)

    fresh = states_of(bmat, x, span_tail)
    pull = states_of(cmat, dy, span_grow)

    half_tokens = tokens // 2
    anywhere = pl.BlockSpec(memory_space=pl.ANY)

    def inner(part, one, two):
        part_values = pl.BlockSpec((half_tokens, wide), lambda g: (part, g))
        part_maps = pl.BlockSpec((half_tokens, STATE), lambda g: (part, g))
        new_values = pl.BlockSpec((half_tokens, wide), lambda g: (0, g))
        new_maps = pl.BlockSpec((half_tokens, STATE), lambda g: (0, g))
        new_rows = pl.BlockSpec((per, half_tokens), lambda g: (g, 0))
        return pl.pallas_call(
            functools.partial(inner_kernel, per=per, size=size),
            grid=(groups,),
            in_specs=[
                part_values, part_values, part_maps, part_maps,
                pl.BlockSpec((per, half_tokens), lambda g: (g, part)),
                pl.BlockSpec((1, half_tokens, per), lambda g: (g, part, 0)),
                anywhere, anywhere,
            ],
            out_specs=[new_values, new_maps, new_maps, new_rows, new_rows],
            out_shape=[
                f32((half_tokens, width)), f32((half_tokens, groups * STATE)),
                f32((half_tokens, groups * STATE)), f32((heads, half_tokens)), f32((heads, half_tokens)),
            ],
            compiler_params=params(),
            cost_estimate=pl.CostEstimate(
                flops=10000000000, bytes_accessed=4 * tokens * width, transcendentals=0
            ),
        )(x, dy, bmat, cmat, cum, off, one, two)

    def advance(one, two, dep):
        return pl.pallas_call(
            step_kernel,
            grid=(groups,),
            in_specs=[pl.BlockSpec((1, wide), lambda g: (0, g)), state, state, state, state, anywhere],
            out_specs=[state, state],
            out_shape=[jax.ShapeDtypeStruct((STATE, width), BF16)] * 2,
            compiler_params=params(),
        )(total, one, fresh, two, pull, dep)

    def hop(value, by):
        pairs = [(i, i + by) for i in range(spans) if 0 <= i + by < spans]
        return lax.ppermute(value, "seq", pairs)

    parts = [None, None]
    if spans > 3:
        back = hop(pull.astype(BF16), -1)
        to_prev = (total * back.astype(F32) + pull).astype(BF16)
        to_next = fresh.astype(BF16)
        back = hop(to_prev, -1)
        ahead = hop(to_next, 1)
        parts[1] = inner(1, to_next, to_prev)
        to_next, to_prev = advance(ahead, back, parts[1][3])
        back = hop(to_prev, -1)
        ahead = hop(to_next, 1)
        parts[0] = inner(0, to_next, to_prev)
        to_next, to_prev = advance(ahead, back, parts[0][3])
        ahead = hop(to_next, 1)
        for _ in range(spans - 4):
            ahead = hop((total * ahead.astype(F32) + fresh).astype(BF16), 1)
            back = hop((total * back.astype(F32) + pull).astype(BF16), -1)
    else:
        ahead = jnp.zeros((STATE, width), BF16)
        back = ahead
        for _ in range(spans - 1):
            ahead = hop((total * ahead.astype(F32) + fresh).astype(BF16), 1)
            back = hop((total * back.astype(F32) + pull).astype(BF16), -1)
        parts = [inner(0, x, x), inner(1, x, x)]

    def outer(part, grad, deps):
        new_values = pl.BlockSpec((half_tokens, wide), lambda g: (0, g))
        new_maps = pl.BlockSpec((half_tokens, STATE), lambda g: (0, g))
        new_rows = pl.BlockSpec((per, half_tokens), lambda g: (g, 0))
        part_maps = pl.BlockSpec((half_tokens, STATE), lambda g: (part, g))
        in_specs = [
            values, values, maps, maps, cols, cols, rows, rows,
            pl.BlockSpec((per, 1), lambda g: (g, 0)),
            state, state, new_values, new_maps, new_maps, new_rows, new_rows,
        ] + [anywhere] * len(deps)
        return pl.pallas_call(
            functools.partial(
                outer_kernel, first=part * chunks // 2, last=(part + 1) * chunks // 2, per=per, size=size
            ),
            grid=(groups,),
            in_specs=in_specs,
            out_specs=[
                new_values, part_maps, part_maps,
                pl.BlockSpec((per, half_tokens), lambda g: (g, part)),
                pl.BlockSpec((per, 128), lambda g: (g, 0)), state,
            ],
            out_shape=[
                jax.ShapeDtypeStruct((half_tokens, width), BF16),
                f32((tokens, groups * STATE)), f32((tokens, groups * STATE)),
                f32((heads, tokens)), f32((heads, 128)), f32((STATE, width)),
            ],
            scratch_shapes=[pltpu.VMEM((chunks, STATE, wide), F32)],
            compiler_params=params(),
            input_output_aliases={16: 1, 17: 2, 18: 3} if deps else {},
            cost_estimate=pl.CostEstimate(
                flops=6000000000, bytes_accessed=8 * tokens * width, transcendentals=0
            ),
        )(
            x, dy, bmat, cmat, tail, grow, growr, steps, decay_rates[:, None], ahead, grad,
            *parts[part], *deps,
        )

    late, grad_b, grad_c, dsteps, late_rates, middle = outer(1, back, [])
    if split == 2:
        weight_own = lax.dynamic_slice_in_dim(in_weight, mine * half, half, 0)
        weight_other = lax.dynamic_slice_in_dim(in_weight, (1 - mine) * half, half, 0)
        late_send = mm(late, weight_other, 1, 1).astype(BF16)
        late_got = lax.ppermute(late_send, "tensor", swap)
    else:
        late_send = late
    early, grad_b, grad_c, dsteps, early_rates, _ = outer(0, middle, [grad_b, grad_c, dsteps, late_send])
    drates = late_rates + early_rates

    if split == 2:
        early_send = mm(early, weight_other, 1, 1).astype(BF16)
        early_got = lax.ppermute(early_send, "tensor", swap)
        late_own = mm(late, weight_own, 1, 1) + late_got.astype(F32)
        early_own = mm(early, weight_own, 1, 1)
        early_own, late_own = lax.optimization_barrier((early_own, late_own))
        grad_inputs = jnp.concatenate(
            [(early_own + early_got.astype(F32)).astype(BF16), late_own.astype(BF16)], axis=0
        )[None]
    else:
        grad_inputs = lax.psum_scatter(
            mm(jnp.concatenate([early, late], axis=0), in_weight, 1, 1), "tensor", scatter_dimension=1, tiled=True
        ).astype(BF16)[None]
    rates = drates[:, 0]
    if lax.axis_size("dp") == 2 and spans == 4:
        rates = rates + lax.ppermute(rates, "dp", [(0, 1), (1, 0)])
        got = [rates]
        for by in range(1, spans):
            got.append(lax.ppermute(rates, "seq", [(i, (i + by) % spans) for i in range(spans)]))
        place = lax.axis_index("seq")
        rate_total = jnp.zeros_like(rates)
        for owner in range(spans):
            away = (place - owner + spans) % spans
            term = got[0]
            for by in range(1, spans):
                term = jnp.where(away == by, got[by], term)
            rate_total = rate_total + term
    else:
        rate_total = lax.psum(rates, ("seq", "dp"))
    return (grad_inputs, grad_b[None], grad_c[None], dsteps[None], rate_total)


def solution(mesh):
    in_specs = (
        P(("groups", "dp"), "seq", "tensor"),
        P(("groups", "dp"), "seq", "tensor"),
        P(("groups", "dp"), "seq"),
        P(("groups", "dp")),
        P(("groups", "dp"), "seq", "tensor"),
        P(("groups", "dp"), "seq", "tensor"),
        P(("groups", "dp"), "tensor", "seq"),
        P("tensor"),
        P(None, "tensor"),
        P("tensor", None),
    )
    out_specs = (
        P(("groups", "dp"), "seq", "tensor"),
        P(("groups", "dp"), "seq", "tensor"),
        P(("groups", "dp"), "seq", "tensor"),
        P(("groups", "dp"), "tensor", "seq"),
        P(("groups", "tensor")),
    )
    return jax.shard_map(local, mesh=mesh, in_specs=in_specs, out_specs=out_specs, check_vma=False)
```

```python
import functools

import jax
import jax.numpy as jnp
from jax import lax
from jax.experimental import pallas as pl
from jax.experimental.pallas import tpu as pltpu
from jax.sharding import PartitionSpec as P

STATE = 128
CHUNK = 128
HIGH = lax.Precision.HIGHEST
F32 = jnp.float32
BF16 = jnp.bfloat16


def mm(a, b, ca=1, cb=0, precision=None):
    return lax.dot_general(
        a, b, (((ca,), (cb,)), ((), ())), preferred_element_type=F32, precision=precision
    )


def head_marks(per, size):
    row = lax.broadcasted_iota(jnp.int32, (per, per * size), 0)
    col = lax.broadcasted_iota(jnp.int32, (per, per * size), 1)
    return (col >= row * size) & (col < row * size + size)


def spread_heads(vals, marks):
    high = vals.astype(BF16)
    low = (vals - high.astype(F32)).astype(BF16)
    return mm(high, marks) + mm(low, marks)


def state_kernel(mat_ref, vals_ref, weight_ref, out_ref, *, per, size):
    marks = head_marks(per, size).astype(F32).astype(BF16)
    scaled = (vals_ref[...].astype(F32) * spread_heads(weight_ref[0], marks)).astype(BF16)
    out_ref[...] = mm(mat_ref[...], scaled, 0, 0)


def inner_kernel(
    x_ref, dy_ref, b_ref, c_ref, cum_ref, off_ref, _one, _two,
    dx_ref, db_ref, dc_ref, dlog_ref, col_ref, *, per, size,
):
    tokens = x_ref.shape[0]
    row = lax.broadcasted_iota(jnp.int32, (CHUNK, CHUNK), 0)
    col = lax.broadcasted_iota(jnp.int32, (CHUNK, CHUNK), 1)
    causal = row <= col
    after = (row >= col).astype(F32)
    ones = jnp.ones((8, CHUNK), BF16)
    head = lax.broadcasted_iota(jnp.int32, (per, CHUNK), 0)
    marks = head_marks(per, CHUNK).astype(F32).astype(BF16)
    pack = 2
    pair_width = pack * size
    lane = lax.broadcasted_iota(jnp.int32, (CHUNK, pair_width), 1)
    left = (lane < size).astype(F32).astype(BF16)
    right = (lane >= size).astype(F32).astype(BF16)

    for chunk in range(tokens // CHUNK):
        at = slice(chunk * CHUNK, (chunk + 1) * CHUNK)
        b = b_ref[at, :]
        c = c_ref[at, :]
        scores = jnp.where(causal, mm(b, c, 1, 1), 0.0)
        dscores = jnp.zeros((CHUNK, CHUNK), F32)
        terms = []
        for j in range(per // pack):
            lanes = slice(j * pair_width, (j + 1) * pair_width)
            x = x_ref[at, lanes]
            dy = dy_ref[at, lanes]
            pairs = mm(jnp.concatenate([x * left, x * right], axis=0), dy, 1, 1)
            weights = []
            for k in range(pack):
                h = j * pack + k
                decay = jnp.exp(cum_ref[h : h + 1, at] + off_ref[0, at, h : h + 1])
                weight = scores * decay
                pair = pairs[k * CHUNK : (k + 1) * CHUNK, :]
                dscores = dscores + pair * decay
                weights.append(weight.astype(BF16))
                terms.append((pair * weight).astype(BF16))
            dx_ref[at, lanes] = mm(
                jnp.concatenate(weights, axis=1), jnp.concatenate([dy * left, dy * right], axis=0)
            )
        terms = jnp.concatenate(terms, axis=0)
        rows = mm(marks, terms)
        sums = mm(ones, terms, 1, 1)
        cols = jnp.zeros((per, CHUNK), F32)
        for h in range(per):
            cols = jnp.where(head == h, sums[:1, h * CHUNK : (h + 1) * CHUNK], cols)
        dscores = jnp.where(causal, dscores, 0.0).astype(BF16)
        db_ref[at, :] = mm(dscores, c)
        dc_ref[at, :] = mm(dscores, b, 0, 0)
        dlog_ref[:, at] = mm(rows - cols, after, precision=HIGH)
        col_ref[:, at] = cols


def step_kernel(total_ref, one_ref, fresh_ref, two_ref, pull_ref, _dep, first_ref, second_ref):
    total = total_ref[...]
    first_ref[...] = (total * one_ref[...].astype(F32) + fresh_ref[...]).astype(BF16)
    second_ref[...] = (total * two_ref[...].astype(F32) + pull_ref[...]).astype(BF16)


def outer_kernel(
    x_ref, dy_ref, b_ref, c_ref, tail_ref, grow_ref, growr_ref, step_ref, rate_ref,
    state_ref, grad_ref, dxi_ref, dbi_ref, dci_ref, dlogi_ref, coli_ref, *rest, first, last, per, size,
):
    dx_ref, db_ref, dc_ref, ds_ref, dr_ref, out_ref, states = rest[-7:]
    row = lax.broadcasted_iota(jnp.int32, (CHUNK, CHUNK), 0)
    col = lax.broadcasted_iota(jnp.int32, (CHUNK, CHUNK), 1)
    after = (row >= col).astype(F32)
    before = (row < col).astype(F32)
    keep = head_marks(per, size)
    marks = keep.astype(F32).astype(BF16)
    rates = rate_ref[...]

    state = state_ref[...].astype(F32)
    for chunk in range(last):
        at = slice(chunk * CHUNK, (chunk + 1) * CHUNK)
        states[chunk] = state
        if chunk < last - 1:
            wx = (x_ref[at, :].astype(F32) * spread_heads(tail_ref[0, at, :], marks)).astype(BF16)
            total = spread_heads(grow_ref[0, (chunk + 1) * CHUNK - 8 : (chunk + 1) * CHUNK, :], marks)
            state = state * total[7:8, :] + mm(b_ref[at, :], wx, 0, 0)

    grad = grad_ref[...].astype(F32)
    rate_sum = jnp.zeros((per, 1), F32)
    for chunk in reversed(range(first, last)):
        at = slice(chunk * CHUNK, (chunk + 1) * CHUNK)
        to = slice((chunk - first) * CHUNK, (chunk - first + 1) * CHUNK)
        b = b_ref[at, :]
        c = c_ref[at, :]
        x = x_ref[at, :].astype(F32)
        tail = spread_heads(tail_ref[0, at, :], marks)
        grow = spread_heads(grow_ref[0, at, :], marks)
        wx = (x * tail).astype(BF16)
        ey = dy_ref[at, :].astype(F32) * grow
        eyb = ey.astype(BF16)
        state = states[chunk]
        stateb = state.astype(BF16)
        gradb = grad.astype(BF16)
        carried = tail * mm(b, gradb)
        dx_ref[to, :] = (dxi_ref[to, :] + carried).astype(BF16)
        cols = mm(marks, (x * carried).astype(BF16), 1, 1)
        rows = mm(marks, (ey * mm(c, stateb)).astype(BF16), 1, 1)
        dc_ref[to, :] = dci_ref[to, :] + mm(eyb, stateb, 1, 1)
        db_ref[to, :] = dbi_ref[to, :] + mm(wx, gradb, 1, 1)
        both = jnp.sum(state * grad, axis=0, keepdims=True)
        both = jnp.sum(jnp.where(keep, both, 0.0), axis=1, keepdims=True)
        total = growr_ref[:, (chunk + 1) * CHUNK - 1 : (chunk + 1) * CHUNK]
        dlog = (
            dlogi_ref[:, to]
            + mm(rows, after, precision=HIGH)
            + mm(cols, before, precision=HIGH)
            + total * both
        )
        steps = step_ref[:, at]
        ds_ref[:, to] = (coli_ref[:, to] + cols) / steps - rates * dlog
        rate_sum = rate_sum - jnp.sum(steps * dlog, axis=1, keepdims=True)
        grad = grad * grow[CHUNK - 1 :, :] + mm(c, eyb, 0, 0)
    dr_ref[...] = jnp.broadcast_to(rate_sum, dr_ref.shape)
    out_ref[...] = grad


def params():
    return pltpu.CompilerParams(vmem_limit_bytes=48 * 1024 * 1024)


def local(
    inputs, targets, active, lengths, b_values, c_values, step_sizes, decay_rates, in_weight, out_weight
):
    tokens = inputs.shape[1]
    width = in_weight.shape[1]
    heads = step_sizes.shape[1]
    size = width // heads
    groups = b_values.shape[2] // STATE
    per = heads // groups
    wide = per * size
    chunks = tokens // CHUNK
    split = lax.axis_size("tensor")
    spans = lax.axis_size("seq")

    position = lax.axis_index("seq") * tokens + jnp.arange(tokens)
    live = (position < lengths[0]) & (active[0] == 1)
    cotan = jnp.where(live[:, None], -targets[0], jnp.zeros_like(targets[0]))
    mine = lax.axis_index("tensor")

    steps = step_sizes[0]
    logs = (-steps * decay_rates[:, None]).reshape(heads, chunks, CHUNK)
    upto = (jnp.arange(CHUNK)[:, None] <= jnp.arange(CHUNK)[None, :]).astype(F32)
    cum3 = jnp.einsum("hct,ts->hcs", logs, upto, precision=HIGH)
    ends = cum3[:, :, -1]
    starts = [jnp.zeros((heads,), F32)]
    for i in range(chunks):
        starts.append(starts[-1] + ends[:, i])
    span3 = cum3 + jnp.stack(starts[:chunks], axis=1)[:, :, None]
    span_end = starts[chunks]
    steps3 = steps.reshape(heads, chunks, CHUNK)

    def columns(value):
        return jnp.transpose(value.reshape(groups, per, tokens), (0, 2, 1))

    cum = cum3.reshape(heads, tokens)
    growr = jnp.exp(cum)
    off = columns(jnp.log(steps3) - cum3)
    tail = columns(jnp.exp(ends[:, :, None] - cum3) * steps3)
    grow = columns(growr)
    span_tail = columns(jnp.exp(span_end[:, None, None] - span3) * steps3)
    span_grow = columns(jnp.exp(span3))
    total = jnp.repeat(jnp.exp(span_end), size)[None, :]

    if split == 2:
        half = inputs.shape[2]
        swap = [(0, 1), (1, 0)]
        other_in = lax.ppermute(inputs[0], "tensor", swap)
        other_cot = lax.ppermute(cotan, "tensor", swap)
        first = mm(inputs[0], lax.dynamic_slice_in_dim(in_weight, mine * half, half, 0))
        second = mm(cotan, lax.dynamic_slice_in_dim(out_weight, mine * half, half, 1), 1, 1)
        first = first + mm(other_in, lax.dynamic_slice_in_dim(in_weight, (1 - mine) * half, half, 0))
        second = second + mm(
            other_cot, lax.dynamic_slice_in_dim(out_weight, (1 - mine) * half, half, 1), 1, 1
        )
    else:
        first = mm(lax.all_gather(inputs[0], "tensor", axis=1, tiled=True), in_weight)
        second = mm(lax.all_gather(cotan, "tensor", axis=1, tiled=True), out_weight, 1, 1)
    x = first.astype(BF16)
    dy = second.astype(BF16)
    bmat = b_values[0]
    cmat = c_values[0]

    values = pl.BlockSpec((tokens, wide), lambda g: (0, g))
    maps = pl.BlockSpec((tokens, STATE), lambda g: (0, g))
    rows = pl.BlockSpec((per, tokens), lambda g: (g, 0))
    cols = pl.BlockSpec((1, tokens, per), lambda g: (g, 0, 0))
    state = pl.BlockSpec((STATE, wide), lambda g: (0, g))
    f32 = functools.partial(jax.ShapeDtypeStruct, dtype=F32)

    def states_of(mat, vals, weight):
        return pl.pallas_call(
            functools.partial(state_kernel, per=per, size=size),
            grid=(groups,),
            in_specs=[maps, values, cols],
            out_specs=state,
            out_shape=f32((STATE, width)),
            compiler_params=params(),
            cost_estimate=pl.CostEstimate(
                flops=2 * tokens * STATE * width, bytes_accessed=4 * tokens * width, transcendentals=0
            ),
        )(mat, vals, weight)

    fresh = states_of(bmat, x, span_tail)
    pull = states_of(cmat, dy, span_grow)

    half_tokens = tokens // 2
    anywhere = pl.BlockSpec(memory_space=pl.ANY)

    def inner(part, one, two):
        part_values = pl.BlockSpec((half_tokens, wide), lambda g: (part, g))
        part_maps = pl.BlockSpec((half_tokens, STATE), lambda g: (part, g))
        new_values = pl.BlockSpec((half_tokens, wide), lambda g: (0, g))
        new_maps = pl.BlockSpec((half_tokens, STATE), lambda g: (0, g))
        new_rows = pl.BlockSpec((per, half_tokens), lambda g: (g, 0))
        return pl.pallas_call(
            functools.partial(inner_kernel, per=per, size=size),
            grid=(groups,),
            in_specs=[
                part_values, part_values, part_maps, part_maps,
                pl.BlockSpec((per, half_tokens), lambda g: (g, part)),
                pl.BlockSpec((1, half_tokens, per), lambda g: (g, part, 0)),
                anywhere, anywhere,
            ],
            out_specs=[new_values, new_maps, new_maps, new_rows, new_rows],
            out_shape=[
                f32((half_tokens, width)), f32((half_tokens, groups * STATE)),
                f32((half_tokens, groups * STATE)), f32((heads, half_tokens)), f32((heads, half_tokens)),
            ],
            compiler_params=params(),
            cost_estimate=pl.CostEstimate(
                flops=10000000000, bytes_accessed=4 * tokens * width, transcendentals=0
            ),
        )(x, dy, bmat, cmat, cum, off, one, two)

    def advance(one, two, dep):
        return pl.pallas_call(
            step_kernel,
            grid=(groups,),
            in_specs=[pl.BlockSpec((1, wide), lambda g: (0, g)), state, state, state, state, anywhere],
            out_specs=[state, state],
            out_shape=[jax.ShapeDtypeStruct((STATE, width), BF16)] * 2,
            compiler_params=params(),
        )(total, one, fresh, two, pull, dep)

    def hop(value, by):
        pairs = [(i, i + by) for i in range(spans) if 0 <= i + by < spans]
        return lax.ppermute(value, "seq", pairs)

    parts = [None, None]
    if spans > 3:
        back = hop(pull.astype(BF16), -1)
        to_prev = (total * back.astype(F32) + pull).astype(BF16)
        to_next = fresh.astype(BF16)
        back = hop(to_prev, -1)
        ahead = hop(to_next, 1)
        parts[1] = inner(1, to_next, to_prev)
        to_next, to_prev = advance(ahead, back, parts[1][3])
        back = hop(to_prev, -1)
        ahead = hop(to_next, 1)
        parts[0] = inner(0, to_next, to_prev)
        to_next, to_prev = advance(ahead, back, parts[0][3])
        ahead = hop(to_next, 1)
        for _ in range(spans - 4):
            ahead = hop((total * ahead.astype(F32) + fresh).astype(BF16), 1)
            back = hop((total * back.astype(F32) + pull).astype(BF16), -1)
    else:
        ahead = jnp.zeros((STATE, width), BF16)
        back = ahead
        for _ in range(spans - 1):
            ahead = hop((total * ahead.astype(F32) + fresh).astype(BF16), 1)
            back = hop((total * back.astype(F32) + pull).astype(BF16), -1)
        parts = [inner(0, x, x), inner(1, x, x)]

    def outer(part, grad, deps):
        new_values = pl.BlockSpec((half_tokens, wide), lambda g: (0, g))
        new_maps = pl.BlockSpec((half_tokens, STATE), lambda g: (0, g))
        new_rows = pl.BlockSpec((per, half_tokens), lambda g: (g, 0))
        part_maps = pl.BlockSpec((half_tokens, STATE), lambda g: (part, g))
        in_specs = [
            values, values, maps, maps, cols, cols, rows, rows,
            pl.BlockSpec((per, 1), lambda g: (g, 0)),
            state, state, new_values, new_maps, new_maps, new_rows, new_rows,
        ] + [anywhere] * len(deps)
        return pl.pallas_call(
            functools.partial(
                outer_kernel, first=part * chunks // 2, last=(part + 1) * chunks // 2, per=per, size=size
            ),
            grid=(groups,),
            in_specs=in_specs,
            out_specs=[
                new_values, part_maps, part_maps,
                pl.BlockSpec((per, half_tokens), lambda g: (g, part)),
                pl.BlockSpec((per, 128), lambda g: (g, 0)), state,
            ],
            out_shape=[
                jax.ShapeDtypeStruct((half_tokens, width), BF16),
                f32((tokens, groups * STATE)), f32((tokens, groups * STATE)),
                f32((heads, tokens)), f32((heads, 128)), f32((STATE, width)),
            ],
            scratch_shapes=[pltpu.VMEM((chunks, STATE, wide), F32)],
            compiler_params=params(),
            input_output_aliases={16: 1, 17: 2, 18: 3} if deps else {},
            cost_estimate=pl.CostEstimate(
                flops=6000000000, bytes_accessed=8 * tokens * width, transcendentals=0
            ),
        )(
            x, dy, bmat, cmat, tail, grow, growr, steps, decay_rates[:, None], ahead, grad,
            *parts[part], *deps,
        )

    late, grad_b, grad_c, dsteps, late_rates, middle = outer(1, back, [])
    if split == 2:
        weight_own = lax.dynamic_slice_in_dim(in_weight, mine * half, half, 0)
        weight_other = lax.dynamic_slice_in_dim(in_weight, (1 - mine) * half, half, 0)
        late_send = mm(late, weight_other, 1, 1).astype(BF16)
        late_got = lax.ppermute(late_send, "tensor", swap)
    else:
        late_send = late
    early, grad_b, grad_c, dsteps, early_rates, _ = outer(0, middle, [grad_b, grad_c, dsteps, late_send])
    drates = late_rates + early_rates

    if split == 2:
        early_send = mm(early, weight_other, 1, 1).astype(BF16)
        late_own = mm(late, weight_own, 1, 1) + late_got.astype(F32)
        after_send, early_send = lax.optimization_barrier((early, early_send))
        early_got = lax.ppermute(early_send, "tensor", swap)
        early_own = mm(after_send, weight_own, 1, 1)
        early_own, late_own = lax.optimization_barrier((early_own, late_own))
        grad_inputs = jnp.concatenate(
            [(early_own + early_got.astype(F32)).astype(BF16), late_own.astype(BF16)], axis=0
        )[None]
    else:
        grad_inputs = lax.psum_scatter(
            mm(jnp.concatenate([early, late], axis=0), in_weight, 1, 1), "tensor", scatter_dimension=1, tiled=True
        ).astype(BF16)[None]
    rates = drates[:, 0]
    if lax.axis_size("dp") == 2 and spans == 4:
        rates = rates + lax.ppermute(rates, "dp", [(0, 1), (1, 0)])
        got = [rates]
        for by in range(1, spans):
            got.append(lax.ppermute(rates, "seq", [(i, (i + by) % spans) for i in range(spans)]))
        place = lax.axis_index("seq")
        rate_total = jnp.zeros_like(rates)
        for owner in range(spans):
            away = (place - owner + spans) % spans
            term = got[0]
            for by in range(1, spans):
                term = jnp.where(away == by, got[by], term)
            rate_total = rate_total + term
    else:
        rate_total = lax.psum(rates, ("seq", "dp"))
    return (grad_inputs, grad_b[None], grad_c[None], dsteps[None], rate_total)


def solution(mesh):
    in_specs = (
        P(("groups", "dp"), "seq", "tensor"),
        P(("groups", "dp"), "seq", "tensor"),
        P(("groups", "dp"), "seq"),
        P(("groups", "dp")),
        P(("groups", "dp"), "seq", "tensor"),
        P(("groups", "dp"), "seq", "tensor"),
        P(("groups", "dp"), "tensor", "seq"),
        P("tensor"),
        P(None, "tensor"),
        P("tensor", None),
    )
    out_specs = (
        P(("groups", "dp"), "seq", "tensor"),
        P(("groups", "dp"), "seq", "tensor"),
        P(("groups", "dp"), "seq", "tensor"),
        P(("groups", "dp"), "tensor", "seq"),
        P(("groups", "tensor")),
    )
    return jax.shard_map(local, mesh=mesh, in_specs=in_specs, out_specs=out_specs, check_vma=False)
```
